32 devices in a mesh: conf: 2 (over x), virt: 16 (over z, y, core).
Axes of the slice: x: 2, y: 2, z: 4, core: 2. Of those that a mesh axis runs over, the one named last changes fastest.
Arguments:
- i_factors: float32 [32, 1024, 2048], P('conf', 'virt'), parts along dimension 0, may hold values from -0.6 to 0.6
- j_factors: float32 [4, 1024, 2048], P('conf', 'virt'), parts along dimension 0, may hold values from -0.6 to 0.6
- occ_i: float32 [32], P('conf'), parts along dimension 0, may hold values from -2 to -0.3
- occ_j: float32 [4], P('conf'), parts along dimension 0, may hold values from -2 to -0.3
- virt_energy: float32 [2048], P(('conf', 'virt')), parts along dimension 0, may hold values from 0.3 to 3
Outputs:
- density: float32 [32, 1024, 2048], P('conf', 'virt'), parts along dimension 0
The draws below stay inside these ranges and needn't reach their ends.
There are 2 independent parts, one for each index of `conf`. The reference program is written for one: setup_inputs(seed, part) draws one part's arguments, and reference() takes and returns one part's arrays. A program takes and returns all parts, laid end to end along the dimension named above; each array names one. Nothing has to cross between parts.
All inputs are finite; a program needn't handle non-finite values.
Results may differ from the reference program's by a relative error of at most 0.00005.
Values sent between devices are 32-bit elements; how exact they have to be, the bound alone decides.
No kernel may reach another device: no remote copies, remote signals or barrier semaphores. Data moves between devices by JAX's collectives and lax.ppermute only.
A program may use at most 128 MiB of HBM per device.

```python
import jax
import jax.numpy as jnp
from jax import lax

NV = 1024
NAUX = 2048
NJ = 2
NI = 16


def level_of(own_key, extent, pieces, least, top_value):
    loudness, own = 1.0, jax.random.fold_in(own_key, 6)
    for dim, blocks in pieces:
        steps = jnp.exp(jax.random.uniform(jax.random.fold_in(own, dim), (blocks,), jnp.float32, least / len(pieces), top_value / len(pieces)))
        loudness = loudness * jnp.repeat(steps, extent[dim] // blocks).reshape([-1 if axis == dim else 1 for axis in range(len(extent))])
    return loudness


def noise(stream_key, shape, spread, most, split=(), kind=jnp.bfloat16):
    array = jax.random.normal(stream_key, shape, jnp.float32) * spread
    if len(split) > 0:
        array = level_of(stream_key, shape, split, -0.22, 0.18) * array
    return jnp.clip(array, min=-most, max=most).astype(kind)


def setup_inputs(seed: int = 0, part: int = 0) -> dict:
    seeds = jax.random.split(jax.random.key(seed), 6)
    own_keys = jax.random.split(jax.random.fold_in(seeds[5], part), 6)
    return {
        "i_factors": noise(own_keys[0], (NI, NV, NAUX), 0.09, 0.6, ((1, 16),), jnp.float32),
        "j_factors": noise(own_keys[1], (NJ, NV, NAUX), 0.09, 0.6, ((1, 16),), jnp.float32),
        "occ_i": jnp.clip(jax.random.uniform(own_keys[2], (NI,), jnp.float32, -2.0, -0.3), -2.0, -0.3),
        "occ_j": jnp.clip(jax.random.uniform(own_keys[3], (NJ,), jnp.float32, -2.0, -0.3), -2.0, -0.3),
        "virt_energy": jnp.clip(0.3 + 2.7 * jax.random.uniform(own_keys[4], (NV,), jnp.float32) ** level_of(own_keys[4], (NV,), ((0, 16),), -0.2, 0.2), 0.3, 3.0),
    }


def reference(i_factors, j_factors, occ_i, occ_j, virt_energy):
    pair = jnp.einsum("iap,jbp->ijab", i_factors, j_factors, precision=lax.Precision.HIGHEST)
    swapped = jnp.swapaxes(pair, 2, 3)
    denominator = (virt_energy[None, None, :, None] + virt_energy[None, None, None, :]
                   - occ_i[:, None, None, None] - occ_j[None, :, None, None])
    amplitude = (swapped - 2.0 * pair) / denominator
    return jnp.einsum("ijab,jbp->iap", amplitude, j_factors, precision=lax.Precision.HIGHEST)
```

```python
import functools

import jax
import jax.numpy as jnp
from jax import lax
from jax.experimental import pallas as pl
from jax.experimental.pallas import tpu as pltpu
from jax.sharding import PartitionSpec as P

AXIS = "virt"
F32 = jnp.float32
BF16 = jnp.bfloat16
MIB = 1 << 20


def halves(x):
    high = x.astype(BF16)
    low = (x - high.astype(F32)).astype(BF16)
    return high, low


def product(left, right, dims):
    one = lambda u, v: lax.dot_general(u, v, (dims, ((), ())), preferred_element_type=F32)
    return one(left[0], right[0]) + (one(left[0], right[1]) + one(left[1], right[0]))


def pair_kernel(count, height, orbitals, left_ref, *refs):
    shard_refs = refs[:count]
    direct_refs = refs[count : 2 * count]
    message_refs = refs[2 * count : 3 * count]
    high_ref, low_ref = refs[3 * count :]
    width = orbitals * height

    @pl.when(pl.program_id(0) == 0)
    def _():
        for spot in range(count):
            rows = pl.ds(spot * width, width)
            high_ref[rows, :], low_ref[rows, :] = halves(shard_refs[spot][...])

    block = product(halves(left_ref[...]), (high_ref[...], low_ref[...]), ((1,), (1,)))
    for spot in range(count):
        part = block[:, spot * width : (spot + 1) * width]
        direct_refs[spot][...] = part
        for row in range(0, part.shape[0], height):
            turned = part[row : row + height].T
            message_refs[spot][row : row + height, :] = jnp.concatenate(
                [turned[j * height : (j + 1) * height] for j in range(orbitals)], axis=1
            )


def pair_blocks(left, shards, height, orbitals):
    count = len(shards)
    rows, depth = left.shape
    width = orbitals * height
    if width % 128 or height % 8:
        direct, messages = [], []
        for shard in shards:
            block = jnp.dot(left, shard.T, precision=lax.Precision.HIGHEST)
            turned = block.reshape(rows // height, height, orbitals, height)
            direct.append(block)
            messages.append(turned.transpose(0, 3, 2, 1).reshape(rows, width))
        return direct, messages
    step = height * min(rows // height, max(1, 256 // height))
    while rows % step:
        step -= height
    out = pl.pallas_call(
        functools.partial(pair_kernel, count, height, orbitals),
        grid=(rows // step,),
        in_specs=[pl.BlockSpec((step, depth), lambda s: (s, 0))]
        + [pl.BlockSpec((width, depth), lambda s: (0, 0))] * count,
        out_specs=[pl.BlockSpec((step, width), lambda s: (s, 0))] * (2 * count),
        out_shape=[jax.ShapeDtypeStruct((rows, width), F32)] * (2 * count),
        scratch_shapes=[pltpu.VMEM((count * width, depth), BF16)] * 2,
        compiler_params=pltpu.CompilerParams(vmem_limit_bytes=32 * MIB),
        cost_estimate=pl.CostEstimate(
            flops=6 * rows * depth * count * width,
            bytes_accessed=4 * (rows * depth + count * width * (depth + 2 * rows)),
            transcendentals=0,
        ),
        name="pair_blocks",
    )(left, *shards)
    return out[:count], out[count:]


def density_kernel(count, first, row_ref, column_ref, *refs):
    direct_refs = refs[:count]
    swapped_refs = refs[count : 2 * count]
    shard_refs = refs[2 * count : 3 * count]
    refs = refs[3 * count :]
    if not first:
        before_ref, *refs = refs
    out_ref, high_ref, low_ref, amp_high_ref, amp_low_ref = refs
    width = direct_refs[0].shape[1]

    @pl.when(pl.program_id(0) == 0)
    def _():
        for spot in range(count):
            rows = pl.ds(spot * width, width)
            high_ref[rows, :], low_ref[rows, :] = halves(shard_refs[spot][...])

    for spot in range(count):
        columns = slice(spot * width, (spot + 1) * width)
        denominator = row_ref[...] + column_ref[:, columns]
        amplitude = (swapped_refs[spot][...] - 2.0 * direct_refs[spot][...]) / denominator
        amp_high_ref[:, columns], amp_low_ref[:, columns] = halves(amplitude)
    total = product(
        (amp_high_ref[...], amp_low_ref[...]), (high_ref[...], low_ref[...]), ((1,), (0,))
    )
    out_ref[...] = total if first else before_ref[...] + total


def density_add(before, row_energy, column_energy, direct, swapped, shards):
    count = len(shards)
    width, depth = shards[0].shape
    rows = row_energy.shape[0]
    if width % 128 or rows % 8:
        for spot in range(count):
            denominator = row_energy + column_energy[:, spot * width : (spot + 1) * width]
            amplitude = (swapped[spot] - 2.0 * direct[spot]) / denominator
            term = jnp.dot(amplitude, shards[spot], precision=lax.Precision.HIGHEST)
            before = term if before is None else before + term
        return before
    step = min(rows, 256)
    while rows % step:
        step -= 8
    first = before is None
    by_rows = lambda columns: pl.BlockSpec((step, columns), lambda s: (s, 0))
    whole = lambda height, columns: pl.BlockSpec((height, columns), lambda s: (0, 0))
    return pl.pallas_call(
        functools.partial(density_kernel, count, first),
        grid=(rows // step,),
        in_specs=[by_rows(1), whole(1, count * width)]
        + [by_rows(width)] * (2 * count)
        + [whole(width, depth)] * count
        + ([] if first else [by_rows(depth)]),
        out_specs=by_rows(depth),
        out_shape=jax.ShapeDtypeStruct((rows, depth), F32),
        scratch_shapes=[pltpu.VMEM((count * width, depth), BF16)] * 2
        + [pltpu.VMEM((step, count * width), BF16)] * 2,
        input_output_aliases={} if first else {2 + 3 * count: 0},
        compiler_params=pltpu.CompilerParams(vmem_limit_bytes=40 * MIB),
        cost_estimate=pl.CostEstimate(
            flops=6 * rows * depth * count * width,
            bytes_accessed=4 * (2 * rows * depth + count * width * (depth + 2 * rows)),
            transcendentals=0,
        ),
        name="density_add",
    )(row_energy, column_energy, *direct, *swapped, *shards, *([] if first else [before]))


def across(x, bits):
    size = lax.axis_size(AXIS)
    return lax.ppermute(x, AXIS, [(i, i ^ bits) for i in range(size)])


def body(i_factors, j_factors, occ_i, occ_j, virt_energy):
    size = lax.axis_size(AXIS)
    orbitals, height, depth = j_factors.shape
    width = orbitals * height
    left = i_factors.reshape(-1, depth)
    own = j_factors.reshape(width, depth)

    padded = jnp.zeros((8, 128 * -(-height // 128)), F32).at[0, :height].set(virt_energy)
    energies = lax.all_gather(padded, AXIS, axis=0)[:, 0, :height]
    place = lax.axis_index(AXIS)
    energies = energies[place ^ jnp.arange(size)]
    row_energy = (virt_energy[None, :] - occ_i[:, None]).reshape(-1, 1)
    column_energy = (energies[:, None, :] - occ_j[None, :, None]).reshape(size, width)

    shards = {0: own}
    for k in sorted(range(2, size, 2), key=lambda k: (bin(k).count("1"), -k)):
        low = k & -k
        shards[k] = across(shards[k ^ low], low)
    for k in range(0, size, 2):
        shards[k + 1] = across(shards[k], 1)

    direct, swapped = {}, {}
    order = sorted(range(0, size, 2), key=lambda k: (bin(k).count("1"), -k))
    for k in order:
        group = (k, k + 1)
        ours, messages = pair_blocks(left, [shards[m] for m in group], height, orbitals)
        for m, one, message in zip(group, ours, messages):
            direct[m] = one
            swapped[m] = across(message, m) if m else message

    density = None
    ready = sorted(range(0, size, 2))
    for k in ready:
        group = (k, k + 1)
        density = density_add(
            density,
            row_energy,
            column_energy[k : k + 2].reshape(1, -1),
            [direct[m] for m in group],
            [swapped[m] for m in group],
            [shards[m] for m in group],
        )
    return density.reshape(i_factors.shape)


def solution(mesh):
    placed = (
        P("conf", "virt", None),
        P("conf", "virt", None),
        P("conf"),
        P("conf"),
        P(("conf", "virt")),
    )
    return jax.shard_map(
        body, mesh=mesh, in_specs=placed, out_specs=P("conf", "virt", None), check_vma=False
    )
```

```python
import functools

import jax
import jax.numpy as jnp
from jax import lax
from jax.experimental import pallas as pl
from jax.experimental.pallas import tpu as pltpu
from jax.sharding import PartitionSpec as P

AXIS = "virt"
F32 = jnp.float32
BF16 = jnp.bfloat16
MIB = 1 << 20
CHEAP = pl.CostEstimate(flops=1, bytes_accessed=1, transcendentals=0)


def halves(x):
    high = x.astype(BF16)
    low = (x - high.astype(F32)).astype(BF16)
    return high, low


def product(left, right, dims):
    one = lambda u, v: lax.dot_general(u, v, (dims, ((), ())), preferred_element_type=F32)
    return one(left[0], right[0]) + (one(left[0], right[1]) + one(left[1], right[0]))


def pair_kernel(count, waits, height, orbitals, left_ref, *refs):
    shard_refs = refs[:count]
    refs = refs[:count] + refs[count + waits :]
    direct_refs = refs[count : 2 * count]
    message_refs = refs[2 * count : 3 * count]
    high_ref, low_ref = refs[3 * count :]
    width = orbitals * height

    @pl.when(pl.program_id(0) == 0)
    def _():
        for spot in range(count):
            rows = pl.ds(spot * width, width)
            high_ref[rows, :], low_ref[rows, :] = halves(shard_refs[spot][...])

    block = product(halves(left_ref[...]), (high_ref[...], low_ref[...]), ((1,), (1,)))
    for spot in range(count):
        part = block[:, spot * width : (spot + 1) * width]
        direct_refs[spot][...] = part
        for row in range(0, part.shape[0], height):
            turned = part[row : row + height].T
            message_refs[spot][row : row + height, :] = jnp.concatenate(
                [turned[j * height : (j + 1) * height] for j in range(orbitals)], axis=1
            )


def pair_blocks(left, shards, height, orbitals, after):
    count = len(shards)
    rows, depth = left.shape
    width = orbitals * height
    if width % 128 or height % 8:
        direct, messages = [], []
        for shard in shards:
            block = jnp.dot(left, shard[:width].T, precision=lax.Precision.HIGHEST)
            turned = block.reshape(rows // height, height, orbitals, height)
            direct.append(block)
            messages.append(turned.transpose(0, 3, 2, 1).reshape(rows, width))
        return direct, messages
    step = height * min(rows // height, max(1, 256 // height))
    while rows % step:
        step -= height
    out = pl.pallas_call(
        functools.partial(pair_kernel, count, len(after), height, orbitals),
        grid=(rows // step,),
        in_specs=[pl.BlockSpec((step, depth), lambda s: (s, 0))]
        + [pl.BlockSpec((width, depth), lambda s: (0, 0))] * count
        + [pl.BlockSpec(memory_space=pl.ANY)] * len(after),
        out_specs=[pl.BlockSpec((step, width), lambda s: (s, 0))] * (2 * count),
        out_shape=[jax.ShapeDtypeStruct((rows, width), F32)] * (2 * count),
        scratch_shapes=[pltpu.VMEM((count * width, depth), BF16)] * 2,
        compiler_params=pltpu.CompilerParams(vmem_limit_bytes=60 * MIB),
        cost_estimate=CHEAP,
        name="pair_blocks",
    )(left, *shards, *after)
    return out[:count], out[count:]


def density_kernel(count, waits, first, row_ref, *refs):
    direct_refs = refs[:count]
    swapped_refs = refs[count : 2 * count]
    shard_refs = refs[2 * count : 3 * count]
    energy_refs = refs[3 * count : 4 * count]
    refs = refs[4 * count + waits :]
    if not first:
        before_ref, *refs = refs
    out_ref, high_ref, low_ref, amp_high_ref, amp_low_ref = refs
    width = direct_refs[0].shape[1]

    @pl.when(pl.program_id(0) == 0)
    def _():
        for spot in range(count):
            rows = pl.ds(spot * width, width)
            high_ref[rows, :], low_ref[rows, :] = halves(shard_refs[spot][...])

    for spot in range(count):
        columns = slice(spot * width, (spot + 1) * width)
        denominator = row_ref[...] + energy_refs[spot][0:1, :]
        amplitude = (swapped_refs[spot][...] - 2.0 * direct_refs[spot][...]) / denominator
        amp_high_ref[:, columns], amp_low_ref[:, columns] = halves(amplitude)
    total = product(
        (amp_high_ref[...], amp_low_ref[...]), (high_ref[...], low_ref[...]), ((1,), (0,))
    )
    out_ref[...] = total if first else before_ref[...] + total


def density_add(before, row_energy, direct, swapped, shards, after):
    count = len(shards)
    rows, width = direct[0].shape
    depth = shards[0].shape[1]
    if width % 128 or rows % 8:
        for spot in range(count):
            denominator = row_energy + shards[spot][width : width + 1, :width]
            amplitude = (swapped[spot] - 2.0 * direct[spot]) / denominator
            term = jnp.dot(amplitude, shards[spot][:width], precision=lax.Precision.HIGHEST)
            before = term if before is None else before + term
        return before
    step = min(rows, 256)
    while rows % step:
        step -= 8
    first = before is None
    by_rows = lambda columns: pl.BlockSpec((step, columns), lambda s: (s, 0))
    whole = lambda height, columns: pl.BlockSpec((height, columns), lambda s: (0, 0))
    return pl.pallas_call(
        functools.partial(density_kernel, count, len(after), first),
        grid=(rows // step,),
        in_specs=[by_rows(1)]
        + [by_rows(width)] * (2 * count)
        + [whole(width, depth)] * count
        + [pl.BlockSpec((8, width), lambda s: (width // 8, 0))] * count
        + [pl.BlockSpec(memory_space=pl.ANY)] * len(after)
        + ([] if first else [by_rows(depth)]),
        out_specs=by_rows(depth),
        out_shape=jax.ShapeDtypeStruct((rows, depth), F32),
        scratch_shapes=[pltpu.VMEM((count * width, depth), BF16)] * 2
        + [pltpu.VMEM((step, count * width), BF16)] * 2,
        input_output_aliases={} if first else {1 + 4 * count + len(after): 0},
        compiler_params=pltpu.CompilerParams(vmem_limit_bytes=60 * MIB),
        cost_estimate=CHEAP,
        name="density_add",
    )(row_energy, *direct, *swapped, *shards, *shards, *after, *([] if first else [before]))


def across(x, bits):
    size = lax.axis_size(AXIS)
    return lax.ppermute(x, AXIS, [(i, i ^ bits) for i in range(size)])


def phases(size):
    far, flat = size // 2, 2
    middle = range(4, far, 4)
    chips = {
        "far": [far],
        "middle": list(middle),
        "flat": [flat],
        "far_middle": [far | m for m in middle],
        "far_flat": [far | flat],
        "middle_flat": [m | flat for m in middle],
        "all": [far | m | flat for m in middle],
        "own": [0],
    }
    pick = lambda *names: [k for name in names for k in chips[name]]
    other = lambda *names: [k + 1 for k in pick(*names)]
    low = lambda k: (k & ~3 & ~far) & -(k & ~3 & ~far)
    cut = lambda kind, ks, most: [(kind, ks[n : n + most]) for n in range(0, len(ks), most)]
    shard = lambda ks, bits: [("shard", k, bits(k)) for k in ks]
    twin = lambda *names: [("twin", k) for k in pick(*names)]
    reply = lambda ks: [("reply", k) for k in ks]
    pair = lambda ks: cut("pair", ks, 2)
    density = lambda ks: cut("density", ks, 4)
    return [
        shard(pick("far"), lambda k: far)
        + shard(pick("middle"), low)
        + shard(pick("flat"), lambda k: flat)
        + twin("own"),
        twin("far", "middle", "flat") + pair(pick("far", "middle")),
        reply(pick("far"))
        + shard(pick("far_flat"), lambda k: flat)
        + shard(pick("far_middle"), low)
        + pair(other("far", "middle"))
        + pair(pick("own", "flat")),
        reply(other("far"))
        + shard(pick("all"), low)
        + shard(pick("middle_flat"), lambda k: flat)
        + twin("far_flat", "far_middle")
        + pair(pick("far_flat", "far_middle")),
        reply(pick("far_flat", "far_middle"))
        + twin("all", "middle_flat")
        + reply(pick("middle"))
        + pair(other("far_flat", "far_middle"))
        + pair(other("own", "flat")),
        reply(other("far_flat", "far_middle"))
        + pair(pick("all", "middle_flat"))
        + pair(other("all", "middle_flat"))
        + reply(other("middle") + pick("all", "middle_flat") + other("all", "middle_flat"))
        + reply([1] + pick("flat") + other("flat"))
        + density(pick("far") + other("far") + pick("far_flat", "far_middle"))
        + density(pick("middle") + other("middle", "far_flat", "far_middle"))
        + density([0, 1] + pick("flat", "middle_flat"))
        + density(pick("all") + other("all", "middle_flat", "flat")),
    ]


def exchange(left, own, row_energy, height, orbitals):
    shards, direct, swapped, messages = {0: own}, {}, {}, {}
    density, last = None, []
    before, now = [], []

    def send(x, bits):
        if before:
            x, _ = lax.optimization_barrier((x, before))
        now.append(across(x, bits))
        return now[-1]

    for steps in phases(lax.axis_size(AXIS)):
        for kind, what, *bits in steps:
            if kind == "shard":
                shards[what] = send(shards[what ^ bits[0]], bits[0])
            elif kind == "twin":
                shards[what + 1] = send(shards[what], 1)
            elif kind == "reply":
                swapped[what] = send(messages[what], what)
            elif kind == "pair":
                waits = [x for x in before if all(x is not y for y in last)]
                ours, theirs = pair_blocks(
                    left, [shards[k] for k in what], height, orbitals, last + waits
                )
                last = [ours[0]]
                for k, one, message in zip(what, ours, theirs):
                    direct[k], messages[k] = one, message
                    if k == 0:
                        swapped[0] = message
            else:
                density = density_add(
                    density,
                    row_energy,
                    [direct[k] for k in what],
                    [swapped[k] for k in what],
                    [shards[k] for k in what],
                    [x for x in last if x is not density],
                )
                last = [density]
        before, now = now + last, []
    return density


def gathered(left, j_factors, row_energy, virt_energy, occ_j, height):
    blocks = lax.axis_size(AXIS)
    total = jnp.zeros(left.shape, F32)
    for index in range(j_factors.shape[0]):
        rows = lax.all_gather(j_factors[index], AXIS, axis=0, tiled=True)
        energy = lax.all_gather(virt_energy, AXIS, axis=0, tiled=True) - occ_j[index]
        pair = jnp.dot(left, rows.T, precision=lax.Precision.HIGHEST)
        split = pair.reshape(-1, height, blocks, height).transpose(0, 3, 2, 1)
        turned = lax.all_to_all(
            split.reshape(-1, height, blocks * height), AXIS, split_axis=2, concat_axis=2, tiled=True
        )
        amplitude = (turned.reshape(pair.shape) - 2.0 * pair) / (row_energy + energy[None, :])
        total = total + jnp.dot(amplitude, rows, precision=lax.Precision.HIGHEST)
    return total


def body(i_factors, j_factors, occ_i, occ_j, virt_energy):
    size = lax.axis_size(AXIS)
    orbitals, height, depth = j_factors.shape
    width = orbitals * height
    left = i_factors.reshape(-1, depth)
    row_energy = (virt_energy[None, :] - occ_i[:, None]).reshape(-1, 1)
    if size < 8 or size & (size - 1) or width > depth:
        density = gathered(left, j_factors, row_energy, virt_energy, occ_j, height)
        return density.reshape(i_factors.shape)
    energy = (virt_energy[None, :] - occ_j[:, None]).reshape(1, width)
    energy = jnp.pad(energy, ((0, 7), (0, depth - width)))
    own = jnp.concatenate([j_factors.reshape(width, depth), energy], axis=0)
    return exchange(left, own, row_energy, height, orbitals).reshape(i_factors.shape)


def solution(mesh):
    placed = (
        P("conf", "virt", None),
        P("conf", "virt", None),
        P("conf"),
        P("conf"),
        P(("conf", "virt")),
    )
    return jax.shard_map(
        body, mesh=mesh, in_specs=placed, out_specs=P("conf", "virt", None), check_vma=False
    )
```

```python
import functools

import jax
import jax.numpy as jnp
from jax import lax
from jax.experimental import pallas as pl
from jax.experimental.pallas import tpu as pltpu
from jax.sharding import PartitionSpec as P

AXIS = "virt"
F32 = jnp.float32
BF16 = jnp.bfloat16
MIB = 1 << 20
CHEAP = pl.CostEstimate(flops=1, bytes_accessed=1, transcendentals=0)


def halves(x):
    high = x.astype(BF16)
    low = (x - high.astype(F32)).astype(BF16)
    return high, low


def product(left, right, dims):
    one = lambda u, v: lax.dot_general(u, v, (dims, ((), ())), preferred_element_type=F32)
    return one(left[0], right[0]) + (one(left[0], right[1]) + one(left[1], right[0]))


def pair_kernel(count, waits, height, orbitals, left_ref, *refs):
    shard_refs = refs[:count]
    refs = refs[:count] + refs[count + waits :]
    direct_refs = refs[count : 2 * count]
    message_refs = refs[2 * count : 3 * count]
    high_ref, low_ref = refs[3 * count :]
    width = orbitals * height

    @pl.when(pl.program_id(0) == 0)
    def _():
        for spot in range(count):
            rows = pl.ds(spot * width, width)
            high_ref[rows, :], low_ref[rows, :] = halves(shard_refs[spot][...])

    block = product(halves(left_ref[...]), (high_ref[...], low_ref[...]), ((1,), (1,)))
    for spot in range(count):
        part = block[:, spot * width : (spot + 1) * width]
        direct_refs[spot][...] = part
        for row in range(0, part.shape[0], height):
            turned = part[row : row + height].T
            message_refs[spot][row : row + height, :] = jnp.concatenate(
                [turned[j * height : (j + 1) * height] for j in range(orbitals)], axis=1
            )


def pair_blocks(left, shards, height, orbitals, after):
    count = len(shards)
    rows, depth = left.shape
    width = orbitals * height
    if width % 128 or height % 8:
        direct, messages = [], []
        for shard in shards:
            block = jnp.dot(left, shard[:width].T, precision=lax.Precision.HIGHEST)
            turned = block.reshape(rows // height, height, orbitals, height)
            direct.append(block)
            messages.append(turned.transpose(0, 3, 2, 1).reshape(rows, width))
        return direct, messages
    step = height * min(rows // height, max(1, 256 // height))
    while rows % step:
        step -= height
    out = pl.pallas_call(
        functools.partial(pair_kernel, count, len(after), height, orbitals),
        grid=(rows // step,),
        in_specs=[pl.BlockSpec((step, depth), lambda s: (s, 0))]
        + [pl.BlockSpec((width, depth), lambda s: (0, 0))] * count
        + [pl.BlockSpec(memory_space=pl.ANY)] * len(after),
        out_specs=[pl.BlockSpec((step, width), lambda s: (s, 0))] * (2 * count),
        out_shape=[jax.ShapeDtypeStruct((rows, width), F32)] * (2 * count),
        scratch_shapes=[pltpu.VMEM((count * width, depth), BF16)] * 2,
        compiler_params=pltpu.CompilerParams(vmem_limit_bytes=60 * MIB),
        cost_estimate=CHEAP,
        name="pair_blocks",
    )(left, *shards, *after)
    return out[:count], out[count:]


def density_kernel(count, waits, first, row_ref, *refs):
    direct_refs = refs[:count]
    swapped_refs = refs[count : 2 * count]
    shard_refs = refs[2 * count : 3 * count]
    energy_refs = refs[3 * count : 4 * count]
    refs = refs[4 * count + waits :]
    if not first:
        before_ref, *refs = refs
    out_ref, high_ref, low_ref, amp_high_ref, amp_low_ref = refs
    width = direct_refs[0].shape[1]

    @pl.when(pl.program_id(0) == 0)
    def _():
        for spot in range(count):
            rows = pl.ds(spot * width, width)
            high_ref[rows, :], low_ref[rows, :] = halves(shard_refs[spot][...])

    for spot in range(count):
        columns = slice(spot * width, (spot + 1) * width)
        denominator = row_ref[...] + energy_refs[spot][0:1, :]
        amplitude = (swapped_refs[spot][...] - 2.0 * direct_refs[spot][...]) / denominator
        amp_high_ref[:, columns], amp_low_ref[:, columns] = halves(amplitude)
    total = product(
        (amp_high_ref[...], amp_low_ref[...]), (high_ref[...], low_ref[...]), ((1,), (0,))
    )
    out_ref[...] = total if first else before_ref[...] + total


def density_add(before, row_energy, direct, swapped, shards, after):
    count = len(shards)
    rows, width = direct[0].shape
    depth = shards[0].shape[1]
    if width % 128 or rows % 8:
        for spot in range(count):
            denominator = row_energy + shards[spot][width : width + 1, :width]
            amplitude = (swapped[spot] - 2.0 * direct[spot]) / denominator
            term = jnp.dot(amplitude, shards[spot][:width], precision=lax.Precision.HIGHEST)
            before = term if before is None else before + term
        return before
    step = min(rows, 256)
    while rows % step:
        step -= 8
    first = before is None
    by_rows = lambda columns: pl.BlockSpec((step, columns), lambda s: (s, 0))
    whole = lambda height, columns: pl.BlockSpec((height, columns), lambda s: (0, 0))
    return pl.pallas_call(
        functools.partial(density_kernel, count, len(after), first),
        grid=(rows // step,),
        in_specs=[by_rows(1)]
        + [by_rows(width)] * (2 * count)
        + [whole(width, depth)] * count
        + [pl.BlockSpec((8, width), lambda s: (width // 8, 0))] * count
        + [pl.BlockSpec(memory_space=pl.ANY)] * len(after)
        + ([] if first else [by_rows(depth)]),
        out_specs=by_rows(depth),
        out_shape=jax.ShapeDtypeStruct((rows, depth), F32),
        scratch_shapes=[pltpu.VMEM((count * width, depth), BF16)] * 2
        + [pltpu.VMEM((step, count * width), BF16)] * 2,
        input_output_aliases={} if first else {1 + 4 * count + len(after): 0},
        compiler_params=pltpu.CompilerParams(vmem_limit_bytes=60 * MIB),
        cost_estimate=CHEAP,
        name="density_add",
    )(row_energy, *direct, *swapped, *shards, *shards, *after, *([] if first else [before]))


def across(x, bits):
    size = lax.axis_size(AXIS)
    return lax.ppermute(x, AXIS, [(i, i ^ bits) for i in range(size)])


def phases(size):
    far, flat = size // 2, 2
    middle = range(4, far, 4)
    chips = {
        "far": [far],
        "middle": list(middle),
        "flat": [flat],
        "far_middle": [far | m for m in middle],
        "far_flat": [far | flat],
        "middle_flat": [m | flat for m in middle],
        "all": [far | m | flat for m in middle],
        "own": [0],
    }
    pick = lambda *names: [k for name in names for k in chips[name]]
    other = lambda *names: [k + 1 for k in pick(*names)]
    low = lambda k: (k & ~3 & ~far) & -(k & ~3 & ~far)
    cut = lambda kind, ks, most: [(kind, ks[n : n + most]) for n in range(0, len(ks), most)]
    shard = lambda ks, bits: [("shard", k, bits(k)) for k in ks]
    twin = lambda *names: [("twin", k) for k in pick(*names)]
    reply = lambda ks: [("reply", k) for k in ks]
    pair = lambda ks: cut("pair", ks, 2)
    density = lambda ks: cut("density", ks, 4)
    return [
        shard(pick("far"), lambda k: far)
        + shard(pick("middle"), low)
        + shard(pick("flat"), lambda k: flat)
        + twin("own"),
        twin("far", "middle", "flat") + pair(pick("far", "middle")),
        reply(pick("far"))
        + shard(pick("far_flat"), lambda k: flat)
        + shard(pick("far_middle"), low)
        + pair(other("far", "middle"))
        + pair(pick("own", "flat")),
        reply(other("far"))
        + shard(pick("all"), low)
        + shard(pick("middle_flat"), lambda k: flat)
        + twin("far_flat", "far_middle")
        + pair(pick("far_flat", "far_middle")),
        reply(pick("far_flat", "far_middle"))
        + twin("all", "middle_flat")
        + reply(pick("middle"))
        + pair(other("far_flat", "far_middle"))
        + pair(other("own", "flat"))
        + density(pick("far") + other("far") + [0]),
        reply(other("far_flat", "far_middle"))
        + pair(pick("all", "middle_flat"))
        + density(pick("far_flat", "far_middle", "middle"))
        + pair(other("all", "middle_flat"))
        + reply(other("middle") + pick("all", "middle_flat") + other("all", "middle_flat"))
        + reply([1] + pick("flat") + other("flat"))
        + density(other("far_flat", "far_middle", "middle"))
        + density(pick("all", "middle_flat", "flat"))
        + density(other("all", "middle_flat", "own", "flat")),
    ]


def exchange(left, own, row_energy, height, orbitals):
    shards, direct, swapped, messages = {0: own}, {}, {}, {}
    density, last = None, []
    before, now = [], []

    def send(x, bits):
        if before:
            x, _ = lax.optimization_barrier((x, before))
        now.append(across(x, bits))
        return now[-1]

    for steps in phases(lax.axis_size(AXIS)):
        for kind, what, *bits in steps:
            if kind == "shard":
                shards[what] = send(shards[what ^ bits[0]], bits[0])
            elif kind == "twin":
                shards[what + 1] = send(shards[what], 1)
            elif kind == "reply":
                swapped[what] = send(messages[what], what)
            elif kind == "pair":
                waits = [x for x in before if all(x is not y for y in last)]
                ours, theirs = pair_blocks(
                    left, [shards[k] for k in what], height, orbitals, last + waits
                )
                last = [ours[0]]
                for k, one, message in zip(what, ours, theirs):
                    direct[k], messages[k] = one, message
                    if k == 0:
                        swapped[0] = message
            else:
                density = density_add(
                    density,
                    row_energy,
                    [direct[k] for k in what],
                    [swapped[k] for k in what],
                    [shards[k] for k in what],
                    [x for x in last if x is not density],
                )
                last = [density]
        before, now = now + last, []
    return density


def gathered(left, j_factors, row_energy, virt_energy, occ_j, height):
    blocks = lax.axis_size(AXIS)
    total = jnp.zeros(left.shape, F32)
    for index in range(j_factors.shape[0]):
        rows = lax.all_gather(j_factors[index], AXIS, axis=0, tiled=True)
        energy = lax.all_gather(virt_energy, AXIS, axis=0, tiled=True) - occ_j[index]
        pair = jnp.dot(left, rows.T, precision=lax.Precision.HIGHEST)
        split = pair.reshape(-1, height, blocks, height).transpose(0, 3, 2, 1)
        turned = lax.all_to_all(
            split.reshape(-1, height, blocks * height), AXIS, split_axis=2, concat_axis=2, tiled=True
        )
        amplitude = (turned.reshape(pair.shape) - 2.0 * pair) / (row_energy + energy[None, :])
        total = total + jnp.dot(amplitude, rows, precision=lax.Precision.HIGHEST)
    return total


def body(i_factors, j_factors, occ_i, occ_j, virt_energy):
    size = lax.axis_size(AXIS)
    orbitals, height, depth = j_factors.shape
    width = orbitals * height
    left = i_factors.reshape(-1, depth)
    row_energy = (virt_energy[None, :] - occ_i[:, None]).reshape(-1, 1)
    if size < 8 or size & (size - 1) or width > depth:
        density = gathered(left, j_factors, row_energy, virt_energy, occ_j, height)
        return density.reshape(i_factors.shape)
    energy = (virt_energy[None, :] - occ_j[:, None]).reshape(1, width)
    energy = jnp.pad(energy, ((0, 7), (0, depth - width)))
    own = jnp.concatenate([j_factors.reshape(width, depth), energy], axis=0)
    return exchange(left, own, row_energy, height, orbitals).reshape(i_factors.shape)


def solution(mesh):
    placed = (
        P("conf", "virt", None),
        P("conf", "virt", None),
        P("conf"),
        P("conf"),
        P(("conf", "virt")),
    )
    return jax.shard_map(
        body, mesh=mesh, in_specs=placed, out_specs=P("conf", "virt", None), check_vma=False
    )
```

```python
import functools

import jax
import jax.numpy as jnp
from jax import lax
from jax.experimental import pallas as pl
from jax.experimental.pallas import tpu as pltpu
from jax.sharding import PartitionSpec as P

AXIS = "virt"
F32 = jnp.float32
BF16 = jnp.bfloat16
MIB = 1 << 20
CHEAP = pl.CostEstimate(flops=1, bytes_accessed=1, transcendentals=0)


def halves(x):
    high = x.astype(BF16)
    low = (x - high.astype(F32)).astype(BF16)
    return high, low


def product(left, right, dims):
    one = lambda u, v: lax.dot_general(u, v, (dims, ((), ())), preferred_element_type=F32)
    return one(left[0], right[0]) + (one(left[0], right[1]) + one(left[1], right[0]))


def pair_kernel(count, waits, height, orbitals, left_ref, *refs):
    shard_refs = refs[:count]
    refs = refs[:count] + refs[count + waits :]
    direct_refs = refs[count : 2 * count]
    message_refs = refs[2 * count : 3 * count]
    high_ref, low_ref = refs[3 * count :]
    width = orbitals * height

    @pl.when(pl.program_id(0) == 0)
    def _():
        for spot in range(count):
            rows = pl.ds(spot * width, width)
            high_ref[rows, :], low_ref[rows, :] = halves(shard_refs[spot][...])

    block = product(halves(left_ref[...]), (high_ref[...], low_ref[...]), ((1,), (1,)))
    for spot in range(count):
        part = block[:, spot * width : (spot + 1) * width]
        direct_refs[spot][...] = part
        for row in range(0, part.shape[0], height):
            turned = part[row : row + height].T
            message_refs[spot][row : row + height, :] = jnp.concatenate(
                [turned[j * height : (j + 1) * height] for j in range(orbitals)], axis=1
            )


def pair_blocks(left, shards, height, orbitals, after):
    count = len(shards)
    rows, depth = left.shape
    width = orbitals * height
    if width % 128 or height % 8:
        direct, messages = [], []
        for shard in shards:
            block = jnp.dot(left, shard[:width].T, precision=lax.Precision.HIGHEST)
            turned = block.reshape(rows // height, height, orbitals, height)
            direct.append(block)
            messages.append(turned.transpose(0, 3, 2, 1).reshape(rows, width))
        return direct, messages
    step = height * min(rows // height, max(1, 256 // height))
    while rows % step:
        step -= height
    out = pl.pallas_call(
        functools.partial(pair_kernel, count, len(after), height, orbitals),
        grid=(rows // step,),
        in_specs=[pl.BlockSpec((step, depth), lambda s: (s, 0))]
        + [pl.BlockSpec((width, depth), lambda s: (0, 0))] * count
        + [pl.BlockSpec(memory_space=pl.ANY)] * len(after),
        out_specs=[pl.BlockSpec((step, width), lambda s: (s, 0))] * (2 * count),
        out_shape=[jax.ShapeDtypeStruct((rows, width), F32)] * (2 * count),
        scratch_shapes=[pltpu.VMEM((count * width, depth), BF16)] * 2,
        compiler_params=pltpu.CompilerParams(vmem_limit_bytes=60 * MIB),
        cost_estimate=CHEAP,
        name="pair_blocks",
    )(left, *shards, *after)
    return out[:count], out[count:]


def density_kernel(count, waits, first, row_ref, *refs):
    direct_refs = refs[:count]
    swapped_refs = refs[count : 2 * count]
    shard_refs = refs[2 * count : 3 * count]
    energy_refs = refs[3 * count : 4 * count]
    refs = refs[4 * count + waits :]
    if not first:
        before_ref, *refs = refs
    out_ref, high_ref, low_ref, amp_high_ref, amp_low_ref = refs
    width = direct_refs[0].shape[1]

    @pl.when(pl.program_id(0) == 0)
    def _():
        for spot in range(count):
            rows = pl.ds(spot * width, width)
            high_ref[rows, :], low_ref[rows, :] = halves(shard_refs[spot][...])

    for spot in range(count):
        columns = slice(spot * width, (spot + 1) * width)
        denominator = row_ref[...] + energy_refs[spot][0:1, :]
        amplitude = (swapped_refs[spot][...] - 2.0 * direct_refs[spot][...]) / denominator
        amp_high_ref[:, columns], amp_low_ref[:, columns] = halves(amplitude)
    total = product(
        (amp_high_ref[...], amp_low_ref[...]), (high_ref[...], low_ref[...]), ((1,), (0,))
    )
    out_ref[...] = total if first else before_ref[...] + total


def density_add(before, row_energy, direct, swapped, shards, after):
    count = len(shards)
    rows, width = direct[0].shape
    depth = shards[0].shape[1]
    if width % 128 or rows % 8:
        for spot in range(count):
            denominator = row_energy + shards[spot][width : width + 1, :width]
            amplitude = (swapped[spot] - 2.0 * direct[spot]) / denominator
            term = jnp.dot(amplitude, shards[spot][:width], precision=lax.Precision.HIGHEST)
            before = term if before is None else before + term
        return before
    step = min(rows, 256)
    while rows % step:
        step -= 8
    first = before is None
    by_rows = lambda columns: pl.BlockSpec((step, columns), lambda s: (s, 0))
    whole = lambda height, columns: pl.BlockSpec((height, columns), lambda s: (0, 0))
    return pl.pallas_call(
        functools.partial(density_kernel, count, len(after), first),
        grid=(rows // step,),
        in_specs=[by_rows(1)]
        + [by_rows(width)] * (2 * count)
        + [whole(width, depth)] * count
        + [pl.BlockSpec((8, width), lambda s: (width // 8, 0))] * count
        + [pl.BlockSpec(memory_space=pl.ANY)] * len(after)
        + ([] if first else [by_rows(depth)]),
        out_specs=by_rows(depth),
        out_shape=jax.ShapeDtypeStruct((rows, depth), F32),
        scratch_shapes=[pltpu.VMEM((count * width, depth), BF16)] * 2
        + [pltpu.VMEM((step, count * width), BF16)] * 2,
        input_output_aliases={} if first else {1 + 4 * count + len(after): 0},
        compiler_params=pltpu.CompilerParams(vmem_limit_bytes=60 * MIB),
        cost_estimate=CHEAP,
        name="density_add",
    )(row_energy, *direct, *swapped, *shards, *shards, *after, *([] if first else [before]))


def across(x, bits):
    size = lax.axis_size(AXIS)
    return lax.ppermute(x, AXIS, [(i, i ^ bits) for i in range(size)])


def phases(size):
    far, flat = size // 2, 2
    middle = range(4, far, 4)
    chips = {
        "far": [far],
        "middle": list(middle),
        "flat": [flat],
        "far_middle": [far | m for m in middle],
        "far_flat": [far | flat],
        "middle_flat": [m | flat for m in middle],
        "all": [far | m | flat for m in middle],
        "own": [0],
    }
    pick = lambda *names: [k for name in names for k in chips[name]]
    other = lambda *names: [k + 1 for k in pick(*names)]
    low = lambda k: (k & ~3 & ~far) & -(k & ~3 & ~far)
    cut = lambda kind, ks, most: [(kind, ks[n : n + most]) for n in range(0, len(ks), most)]
    shard = lambda ks, bits: [("shard", k, bits(k)) for k in ks]
    twin = lambda *names: [("twin", k) for k in pick(*names)]
    reply = lambda ks: [("reply", k) for k in ks]
    pair = lambda ks: cut("pair", ks, 2)
    density = lambda ks: cut("density", ks, 4)
    return [
        shard(pick("far"), lambda k: far)
        + shard(pick("middle"), low)
        + shard(pick("flat"), lambda k: flat)
        + twin("own"),
        twin("far", "middle", "flat") + pair(pick("far")),
        reply(pick("far"))
        + shard(pick("far_flat"), lambda k: flat)
        + shard(pick("far_middle"), low)
        + pair(other("far", "middle"))
        + pair(pick("own", "flat"))
        + pair(pick("middle")),
        reply(other("far"))
        + shard(pick("all"), low)
        + shard(pick("middle_flat"), lambda k: flat)
        + twin("far_flat", "far_middle")
        + pair(pick("far_flat", "far_middle")),
        reply(pick("far_flat", "far_middle"))
        + twin("all", "middle_flat")
        + reply(pick("middle"))
        + pair(other("far_flat", "far_middle"))
        + pair(other("own", "flat"))
        + density(pick("far") + other("far") + [0]),
        reply(other("far_flat", "far_middle"))
        + pair(pick("all", "middle_flat"))
        + density(pick("far_flat", "far_middle", "middle"))
        + pair(other("all", "middle_flat"))
        + reply(other("middle") + pick("all", "middle_flat") + other("all", "middle_flat"))
        + reply([1] + pick("flat") + other("flat"))
        + density(other("far_flat", "far_middle", "middle"))
        + density(pick("all", "middle_flat", "flat"))
        + density(other("all", "middle_flat", "own", "flat")),
    ]


def exchange(left, own, row_energy, height, orbitals):
    shards, direct, swapped, messages = {0: own}, {}, {}, {}
    density, last = None, []
    before, now = [], []

    def send(x, bits):
        if before:
            x, _ = lax.optimization_barrier((x, before))
        now.append(across(x, bits))
        return now[-1]

    for steps in phases(lax.axis_size(AXIS)):
        for kind, what, *bits in steps:
            if kind == "shard":
                shards[what] = send(shards[what ^ bits[0]], bits[0])
            elif kind == "twin":
                shards[what + 1] = send(shards[what], 1)
            elif kind == "reply":
                swapped[what] = send(messages[what], what)
            elif kind == "pair":
                waits = [x for x in before if all(x is not y for y in last)]
                ours, theirs = pair_blocks(
                    left, [shards[k] for k in what], height, orbitals, last + waits
                )
                last = [ours[0]]
                for k, one, message in zip(what, ours, theirs):
                    direct[k], messages[k] = one, message
                    if k == 0:
                        swapped[0] = message
            else:
                density = density_add(
                    density,
                    row_energy,
                    [direct[k] for k in what],
                    [swapped[k] for k in what],
                    [shards[k] for k in what],
                    [x for x in last if x is not density],
                )
                last = [density]
        before, now = now + last, []
    return density


def gathered(left, j_factors, row_energy, virt_energy, occ_j, height):
    blocks = lax.axis_size(AXIS)
    total = jnp.zeros(left.shape, F32)
    for index in range(j_factors.shape[0]):
        rows = lax.all_gather(j_factors[index], AXIS, axis=0, tiled=True)
        energy = lax.all_gather(virt_energy, AXIS, axis=0, tiled=True) - occ_j[index]
        pair = jnp.dot(left, rows.T, precision=lax.Precision.HIGHEST)
        split = pair.reshape(-1, height, blocks, height).transpose(0, 3, 2, 1)
        turned = lax.all_to_all(
            split.reshape(-1, height, blocks * height), AXIS, split_axis=2, concat_axis=2, tiled=True
        )
        amplitude = (turned.reshape(pair.shape) - 2.0 * pair) / (row_energy + energy[None, :])
        total = total + jnp.dot(amplitude, rows, precision=lax.Precision.HIGHEST)
    return total


def body(i_factors, j_factors, occ_i, occ_j, virt_energy):
    size = lax.axis_size(AXIS)
    orbitals, height, depth = j_factors.shape
    width = orbitals * height
    left = i_factors.reshape(-1, depth)
    row_energy = (virt_energy[None, :] - occ_i[:, None]).reshape(-1, 1)
    if size < 8 or size & (size - 1) or width > depth:
        density = gathered(left, j_factors, row_energy, virt_energy, occ_j, height)
        return density.reshape(i_factors.shape)
    energy = (virt_energy[None, :] - occ_j[:, None]).reshape(1, width)
    energy = jnp.pad(energy, ((0, 7), (0, depth - width)))
    own = jnp.concatenate([j_factors.reshape(width, depth), energy], axis=0)
    return exchange(left, own, row_energy, height, orbitals).reshape(i_factors.shape)


def solution(mesh):
    placed = (
        P("conf", "virt", None),
        P("conf", "virt", None),
        P("conf"),
        P("conf"),
        P(("conf", "virt")),
    )
    return jax.shard_map(
        body, mesh=mesh, in_specs=placed, out_specs=P("conf", "virt", None), check_vma=False
    )
```
